256 devices in a mesh: seq: 64 (over y, z, core), mp: 4 (over x).
Axes of the slice: x: 4, y: 4, z: 8, core: 2. Of those that a mesh axis runs over, the one named last changes fastest.
Arguments:
- query: bfloat16 [16384, 8192], P('seq', 'mp'), may hold values from -5 to 5
- image_key_values: bfloat16 [2, 64, 64, 1024], P(None, 'seq', 'mp'), may hold values from -5 to 5
- image_count: int32 [64], P('seq'), may hold values from 2 to 64, as said below
- block_images: int32 [128, 6], P('seq'), may hold values from 0 to 63, as said below
- block_reads: int32 [128], P('seq'), may hold values from 3 to 6
- output_gradient: bfloat16 [16384, 8192], P('seq', 'mp'), may hold values from -6 to 6
Outputs:
- attended: bfloat16 [16384, 8192], P('seq', 'mp')
- grad_query: bfloat16 [16384, 8192], P('seq', 'mp')
- grad_kv: float32 [2, 64, 64, 1024], P(None, 'seq', 'mp')
The draws below stay inside these ranges and needn't reach their ends.
Inputs may be any that keep to these rules, and one draw needn't show every extreme that they name: Slots j >= image_count[i] of image i hold padding. `block_images`: the ids in one row are different; only the first block_reads[b] entries of row b are read.
All inputs are finite; a program needn't handle non-finite values.
Results may differ from the reference program's by a relative error of at most 0.03.
Values may be sent and summed in bfloat16 or wider, within the bound.
No kernel may reach another device: no remote copies, remote signals or barrier semaphores. Data moves between devices by JAX's collectives and lax.ppermute only.
A program may use at most 128 MiB of HBM per device.

```python
import jax
import jax.numpy as jnp
from jax import lax

QUERY_HEADS = 64
KEY_VALUE_HEADS = 8
HEAD_WIDTH = 128
BLOCK_TEXT_ROWS = 128
IMAGE_TOKENS = 64
MAX_BLOCK_READS = 6
TOKENS = 16384
TEXT_BLOCK_COUNT = 128
IMAGE_TOTAL = 64


def draw_query(key, part):
    key = jax.random.fold_in(key, 1)
    base_offset = jnp.clip(jax.random.normal(key, (TOKENS, QUERY_HEADS * HEAD_WIDTH), jnp.float32), -5.0, 5.0)
    return base_offset.astype(jnp.bfloat16)


def draw_image_key_values(key, part):
    key = jax.random.fold_in(key, 2)
    base_offset = jnp.clip(jax.random.normal(key, (2, IMAGE_TOTAL, IMAGE_TOKENS, KEY_VALUE_HEADS * HEAD_WIDTH), jnp.float32), -5.0, 5.0)
    return base_offset.astype(jnp.bfloat16)


def draw_image_count(key, part):
    key = jax.random.fold_in(key, 3)
    counts = jax.random.randint(key, (IMAGE_TOTAL,), 2, IMAGE_TOKENS + 1)
    spot = jax.random.randint(jax.random.fold_in(key, 1), (), 0, IMAGE_TOTAL)
    return jnp.where(jnp.arange(IMAGE_TOTAL) == spot, IMAGE_TOKENS, counts).astype(jnp.int32)


def draw_block_images(key, part):
    key = jax.random.fold_in(key, 4)
    scores = jax.random.randint(key, (TEXT_BLOCK_COUNT, IMAGE_TOTAL), 0, 2 ** 20) * IMAGE_TOTAL + jnp.arange(IMAGE_TOTAL)[None, :]
    order = jnp.argsort(scores, axis=1)
    return order[:, :MAX_BLOCK_READS].astype(jnp.int32)


def draw_block_reads(key, part):
    key = jax.random.fold_in(key, 5)
    reads = jax.random.randint(key, (TEXT_BLOCK_COUNT,), MAX_BLOCK_READS // 2, MAX_BLOCK_READS + 1)
    spot = jax.random.randint(jax.random.fold_in(key, 1), (), 0, TEXT_BLOCK_COUNT)
    return jnp.where(jnp.arange(TEXT_BLOCK_COUNT) == spot, MAX_BLOCK_READS, reads).astype(jnp.int32)


def steps_of(stream_key, shape, cuts, least, top_value):
    loudness, own = 1.0, jax.random.fold_in(stream_key, 6)
    for dim, parts in cuts:
        heights = jnp.exp(jax.random.uniform(jax.random.fold_in(own, dim), (parts,), jnp.float32, least / len(cuts), top_value / len(cuts)))
        loudness = loudness * jnp.repeat(heights, shape[dim] // parts).reshape([-1 if axis == dim else 1 for axis in range(len(shape))])
    return loudness


def gaussian(rng, dims, scale, reach, pieces=(), kind=jnp.bfloat16):
    entries = scale * jax.random.normal(rng, dims, jnp.float32)
    if pieces:
        entries = entries * steps_of(rng, dims, pieces, -0.22, 0.18)
    return jnp.clip(entries, -reach, reach).astype(kind)


def setup_inputs(seed: int = 0) -> dict:
    seeds = jax.random.split(jax.random.key(seed), 7)
    query = draw_query(jax.random.fold_in(seeds[6], 71), 0)
    image_key_values = draw_image_key_values(jax.random.fold_in(seeds[6], 71), 0)
    image_count = draw_image_count(jax.random.fold_in(seeds[6], 71), 0)
    block_images = draw_block_images(jax.random.fold_in(seeds[6], 71), 0)
    block_reads = draw_block_reads(jax.random.fold_in(seeds[6], 71), 0)
    output_gradient = gaussian(seeds[5], (TOKENS, QUERY_HEADS * HEAD_WIDTH), 1.0, 6.0, ((0, 64), (1, 4)))
    return {"query": query, "image_key_values": image_key_values, "image_count": image_count, "block_images": block_images, "block_reads": block_reads, "output_gradient": output_gradient}


def attend(q_block, g_block, image_indices, reads, image_key_values, valid_tok):
    head_group = QUERY_HEADS // KEY_VALUE_HEADS
    scale = HEAD_WIDTH ** -0.5
    image_keys = image_key_values[0][image_indices].reshape(MAX_BLOCK_READS * IMAGE_TOKENS, KEY_VALUE_HEADS, HEAD_WIDTH).astype(jnp.float32)
    image_values = image_key_values[1][image_indices].reshape(MAX_BLOCK_READS * IMAGE_TOKENS, KEY_VALUE_HEADS, HEAD_WIDTH).astype(jnp.float32)
    live = (jnp.arange(MAX_BLOCK_READS, dtype=jnp.int32)[:, None] < reads) & valid_tok[image_indices]
    live = live.reshape(MAX_BLOCK_READS * IMAGE_TOKENS)
    q_f = q_block.astype(jnp.float32)
    g_f = g_block.astype(jnp.float32)
    scores = jnp.einsum("tgad,lgd->gatl", q_f, image_keys) * scale
    scores = jnp.where(live, scores, -jnp.inf)
    top = jnp.max(scores, axis=-1, keepdims=True)
    expo = jnp.exp(scores - top)
    probs = expo / jnp.sum(expo, axis=-1, keepdims=True)
    probs_b = probs.astype(jnp.bfloat16)
    attention_output = jnp.einsum("gatl,lgd->tgad", probs_b.astype(jnp.float32), image_values).astype(jnp.bfloat16)
    delta = jnp.einsum("tgad,tgad->gat", g_f, attention_output.astype(jnp.float32))
    dprobs = jnp.einsum("tgad,lgd->gatl", g_f, image_values)
    dscores = (probs * (dprobs - delta[..., None]) * scale).astype(jnp.bfloat16)
    query_gradient = jnp.einsum("gatl,lgd->tgad", dscores.astype(jnp.float32), image_keys).astype(jnp.bfloat16)
    key_gradient = jnp.einsum("gatl,tgad->lgd", dscores.astype(jnp.float32), q_f)
    value_gradient = jnp.einsum("gatl,tgad->lgd", probs_b.astype(jnp.float32), g_f)
    return attention_output, query_gradient, key_gradient.reshape(MAX_BLOCK_READS, IMAGE_TOKENS, KEY_VALUE_HEADS * HEAD_WIDTH), value_gradient.reshape(MAX_BLOCK_READS, IMAGE_TOKENS, KEY_VALUE_HEADS * HEAD_WIDTH)


def reference(query, image_key_values, image_count, block_images, block_reads, output_gradient):
    head_group = QUERY_HEADS // KEY_VALUE_HEADS
    valid_tok = jnp.arange(IMAGE_TOKENS, dtype=jnp.int32)[None, :] < image_count[:, None]
    query_blocks = query.reshape(TEXT_BLOCK_COUNT, BLOCK_TEXT_ROWS, KEY_VALUE_HEADS, head_group, HEAD_WIDTH)
    gradient_blocks = output_gradient.reshape(TEXT_BLOCK_COUNT, BLOCK_TEXT_ROWS, KEY_VALUE_HEADS, head_group, HEAD_WIDTH)

    def step(total, item):
        q_block, g_block, image_indices, reads = item
        attention_output, query_gradient, key_gradient, value_gradient = attend(q_block, g_block, image_indices, reads, image_key_values, valid_tok)
        total = total.at[0, image_indices].add(key_gradient).at[1, image_indices].add(value_gradient)
        return total, (attention_output, query_gradient)

    start_offset = jnp.zeros((2, IMAGE_TOTAL, IMAGE_TOKENS, KEY_VALUE_HEADS * HEAD_WIDTH), jnp.float32)
    grads, (outs, dqs) = lax.scan(step, start_offset, (query_blocks, gradient_blocks, block_images, block_reads))
    return outs.reshape(TOKENS, QUERY_HEADS * HEAD_WIDTH), dqs.reshape(TOKENS, QUERY_HEADS * HEAD_WIDTH), grads
```

```python
import functools

import jax
import jax.numpy as jnp
import numpy as np
from jax import lax
from jax.experimental import pallas as pl
from jax.experimental.pallas import tpu as pltpu
from jax.sharding import Mesh, PartitionSpec as P

QUERY_HEADS = 64
KEY_VALUE_HEADS = 8
HEAD_WIDTH = 128
MAX_BLOCK_READS = 6
IMAGE_TOKENS = 64
GROUP = QUERY_HEADS // KEY_VALUE_HEADS
ROWS = 128
KEYS = MAX_BLOCK_READS * IMAGE_TOKENS
SCALE = HEAD_WIDTH**-0.5
LOG2E = 1.4426950408889634
MARKER = 2.0**20
DEAD = -1e30
SEQ = ("y", "z", "c")
Z = 8

f32 = jnp.float32
bf16 = jnp.bfloat16


def mm(a, b, ca, cb):
    return lax.dot_general(a, b, (((ca,), (cb,)), ((), ())), preferred_element_type=f32)


def attend_kernel(
    images, reads, pos, q_ref, g_ref, own_ref, sib_ref,
    att_ref, dq_ref, gown_ref, gsib_ref,
    k_s, v_s, kt_s, vt_s, bias_s, dk_s, dv_s,
):
    b = pl.program_id(0)
    h = pl.program_id(1)

    @pl.when((b == 0) & (h == 0))
    def _():
        gown_ref[...] = jnp.zeros(gown_ref.shape, gown_ref.dtype)
        gsib_ref[...] = jnp.zeros(gsib_ref.shape, gsib_ref.dtype)

    places = []
    for r in range(MAX_BLOCK_READS):
        image = images[b, r]
        rel = ((image >> 1) + Z - pos[0]) & (Z - 1)
        places.append(((image & 1) == pos[1], rel, image >> 4))
    for r, (mine, rel, y) in enumerate(places):
        rows = pl.ds(r * IMAGE_TOKENS, IMAGE_TOKENS)

        def fetch(ref, rel=rel, y=y, rows=rows, r=r):
            k = ref[rel, y, :, 0, h].reshape(IMAGE_TOKENS, HEAD_WIDTH).astype(f32)
            dead = k > 0.5 * MARKER
            k_s[rows, :] = jnp.where(dead, 0.0, k).astype(bf16)
            unread = jnp.where(r < reads[b], 0.0, DEAD)
            bias_s[rows, :] = jnp.where(dead, DEAD, unread)
            v_s[rows, :] = ref[rel, y, :, 1, h].reshape(IMAGE_TOKENS, HEAD_WIDTH)

        pl.when(mine)(functools.partial(fetch, own_ref))
        pl.when(jnp.logical_not(mine))(functools.partial(fetch, sib_ref))
    kt_s[...] = k_s[...].T
    vt_s[...] = v_s[...].T

    k, v, kt, vt = k_s[...], v_s[...], kt_s[...], vt_s[...]
    for i in range(GROUP // 2):
        c0, c1, c2 = 2 * i * HEAD_WIDTH, (2 * i + 1) * HEAD_WIDTH, (2 * i + 2) * HEAD_WIDTH
        q2 = jnp.concatenate([q_ref[:, c0:c1], q_ref[:, c1:c2]], axis=0)
        g2 = jnp.concatenate([g_ref[:, c0:c1], g_ref[:, c1:c2]], axis=0)
        bias = bias_s[...]
        t = mm(k, q2, 1, 1) * (SCALE * LOG2E) + jnp.concatenate([bias, bias], axis=1)
        e = jnp.exp2(t - jnp.max(t, axis=0, keepdims=True))
        p = e * (1.0 / jnp.sum(e, axis=0, keepdims=True))
        pb = p.astype(bf16)
        dp = mm(v, g2, 1, 1)
        delta = jnp.sum(p * dp, axis=0, keepdims=True)
        ds = (p * (dp - delta)).astype(bf16)
        o = mm(vt, pb, 1, 0).astype(bf16).T
        dq = (mm(kt, ds, 1, 0) * SCALE).astype(bf16).T
        att_ref[:, c0:c1], att_ref[:, c1:c2] = o[:ROWS], o[ROWS:]
        dq_ref[:, c0:c1], dq_ref[:, c1:c2] = dq[:ROWS], dq[ROWS:]
        dk, dv = mm(ds, q2, 1, 0), mm(pb, g2, 1, 0)
        if i == 0:
            dk_s[...], dv_s[...] = dk, dv
        else:
            dk_s[...] += dk
            dv_s[...] += dv

    for r, (mine, rel, y) in enumerate(places):
        rows = pl.ds(r * IMAGE_TOKENS, IMAGE_TOKENS)

        def add(ref, rel=rel, y=y, rows=rows):
            shape = (4, IMAGE_TOKENS // 4, HEAD_WIDTH)
            dk = (dk_s[rows, :] * SCALE).reshape(shape)
            dv = dv_s[rows, :].reshape(shape)
            ref[rel, y, :, 0, h] = (ref[rel, y, :, 0, h].astype(f32) + dk).astype(bf16)
            ref[rel, y, :, 1, h] = (ref[rel, y, :, 1, h].astype(f32) + dv).astype(bf16)

        pl.when(mine)(functools.partial(add, gown_ref))
        pl.when(jnp.logical_not(mine))(functools.partial(add, gsib_ref))


def attend(images, reads, pos, query, gradient, own, sib):
    blocks = images.shape[0]
    heads = query.shape[1] // (GROUP * HEAD_WIDTH)
    smem = pl.BlockSpec(memory_space=pltpu.SMEM)
    whole = pl.BlockSpec(memory_space=pltpu.VMEM)
    text = pl.BlockSpec((ROWS, GROUP * HEAD_WIDTH), lambda b, h: (b, h))
    pairs = blocks * heads * GROUP * ROWS * KEYS
    return pl.pallas_call(
        attend_kernel,
        grid=(blocks, heads),
        in_specs=[smem, smem, smem, text, text, whole, whole],
        out_specs=[text, text, whole, whole],
        out_shape=[
            jax.ShapeDtypeStruct(query.shape, bf16),
            jax.ShapeDtypeStruct(query.shape, bf16),
            jax.ShapeDtypeStruct(own.shape, bf16),
            jax.ShapeDtypeStruct(own.shape, bf16),
        ],
        scratch_shapes=[
            pltpu.VMEM((KEYS, HEAD_WIDTH), bf16),
            pltpu.VMEM((KEYS, HEAD_WIDTH), bf16),
            pltpu.VMEM((HEAD_WIDTH, KEYS), bf16),
            pltpu.VMEM((HEAD_WIDTH, KEYS), bf16),
            pltpu.VMEM((KEYS, HEAD_WIDTH), f32),
            pltpu.VMEM((KEYS, HEAD_WIDTH), f32),
            pltpu.VMEM((KEYS, HEAD_WIDTH), f32),
        ],
        compiler_params=pltpu.CompilerParams(
            dimension_semantics=("arbitrary", "arbitrary"), vmem_limit_bytes=40 * 2**20
        ),
        cost_estimate=pl.CostEstimate(
            flops=12 * HEAD_WIDTH * pairs, bytes_accessed=12 * 2**20, transcendentals=pairs
        ),
    )(images, reads, pos, query, gradient, own, sib)


def shift(x, axis, size, by):
    return lax.ppermute(x, axis, [(i, (i + by) % size) for i in range(size)])


def gather_z(unit):
    half = unit.shape[0] // 2
    up, down = [unit], [unit]
    for _ in range(3):
        up.append(shift(up[-1], "z", Z, 1))
        down.append(shift(down[-1], "z", Z, -1))
    far = jnp.concatenate([shift(up[3][:half], "z", Z, 1), shift(down[3][half:], "z", Z, -1)])
    return jnp.stack([unit, down[1], down[2], down[3], far, up[3], up[2], up[1]])


def add(a, b):
    return (a.astype(f32) + b.astype(f32)).astype(bf16)


def reduce_z(part):
    half = part.shape[1] // 2
    up = shift(part[4][:half], "z", Z, 1)
    down = shift(part[4][half:], "z", Z, -1)
    up = jnp.concatenate([add(part[3][:half], up), part[3][half:]])
    down = jnp.concatenate([part[5][:half], add(part[5][half:], down)])
    up, down = shift(up, "z", Z, 1), shift(down, "z", Z, -1)
    up, down = shift(add(part[2], up), "z", Z, 1), shift(add(part[6], down), "z", Z, -1)
    up, down = shift(add(part[1], up), "z", Z, 1), shift(add(part[7], down), "z", Z, -1)
    return part[0].astype(f32) + up.astype(f32) + down.astype(f32)


def local(query, image_key_values, image_count, block_images, block_reads, output_gradient):
    z, c = lax.axis_index("z"), lax.axis_index("c")
    slots = image_key_values.shape[2]
    slot = lax.axis_index("mp") * slots + jnp.arange(slots, dtype=jnp.int32)
    dead = (slot >= image_count[0])[None, :, None] & (jnp.arange(2) == 0)[:, None, None]
    kv = jnp.where(dead, MARKER, image_key_values[:, 0]).astype(bf16)
    kv = kv.reshape(2, slots, 4, 2, HEAD_WIDTH).transpose(2, 0, 3, 1, 4)
    kv = jnp.broadcast_to(kv[None], (4,) + kv.shape).reshape((16,) + kv.shape[1:])
    unit = lax.all_to_all(kv, ("y", "mp"), 0, 0, tiled=True)
    unit = unit.reshape((4, 4) + unit.shape[1:])
    own = gather_z(unit)
    sib = shift(own, "c", 2, 1)
    pos = jnp.stack([z, c]).astype(jnp.int32)
    attended, grad_query, gown, gsib = attend(
        block_images, block_reads, pos, query, output_gradient, own, sib
    )
    part = add(gown, shift(gsib, "c", 2, 1))
    total = reduce_z(part).astype(bf16)
    total = total.reshape((16,) + total.shape[2:])
    total = lax.all_to_all(total, ("y", "mp"), 0, 0, tiled=True)
    total = jnp.sum(total.reshape((4, 4) + total.shape[1:]).astype(f32), axis=0)
    grad_kv = total.transpose(1, 3, 0, 2, 4).reshape(image_key_values.shape)
    return attended, grad_query, grad_kv


def solution(mesh):
    fine = Mesh(np.asarray(mesh.devices).reshape(4, Z, 2, 4), SEQ + ("mp",))
    placed = (
        P(SEQ, "mp"),
        P(None, SEQ, "mp", None),
        P(SEQ),
        P(SEQ, None),
        P(SEQ),
        P(SEQ, "mp"),
    )
    return jax.shard_map(
        local,
        mesh=fine,
        in_specs=placed,
        out_specs=(P(SEQ, "mp"), P(SEQ, "mp"), P(None, SEQ, "mp", None)),
        check_vma=False,
    )
```

```python
import functools

import jax
import jax.numpy as jnp
import numpy as np
from jax import lax
from jax.experimental import pallas as pl
from jax.experimental.pallas import tpu as pltpu
from jax.sharding import Mesh, PartitionSpec as P

QUERY_HEADS = 64
KEY_VALUE_HEADS = 8
HEAD_WIDTH = 128
MAX_BLOCK_READS = 6
IMAGE_TOKENS = 64
GROUP = QUERY_HEADS // KEY_VALUE_HEADS
ROWS = 128
KEYS = MAX_BLOCK_READS * IMAGE_TOKENS
SCALE = HEAD_WIDTH**-0.5
LOG2E = 1.4426950408889634
MARKER = 2.0**20
DEAD = -1e30
SEQ = ("y", "z", "c")
Y, Z, M = 4, 8, 4

f32 = jnp.float32
bf16 = jnp.bfloat16


def mm(a, b, ca, cb):
    return lax.dot_general(a, b, (((ca,), (cb,)), ((), ())), preferred_element_type=f32)


def attend_kernel(images, reads, pos, q_ref, g_ref, *refs):
    own, sib = refs[:2], refs[2:4]
    att_ref, dq_ref, gown_ref, gsoon_ref, glate_ref = refs[4:9]
    k_s, v_s, kt_s, vt_s, bias_s, dk_s, dv_s = refs[9:]
    b = pl.program_id(0)
    blocks, heads = dk_s.shape[:2]
    z, c = pos[0], pos[1]

    for r in range(MAX_BLOCK_READS):
        image = images[b, r]
        mine = (image & 1) == c
        rel = ((image >> 1) + Z - z) & (Z - 1)
        late = (rel >= 3) & (rel < 6)
        rows = pl.ds(r * IMAGE_TOKENS, IMAGE_TOKENS)

        def fetch(ref, at, image=image, rows=rows, r=r):
            unread = jnp.where(r < reads[b], 0.0, DEAD)
            for h in range(heads):
                k = ref[at, image >> 4, :, 0, h].reshape(IMAGE_TOKENS, HEAD_WIDTH).astype(f32)
                dead = k > 0.5 * MARKER
                k_s[h, rows, :] = jnp.where(dead, 0.0, k).astype(bf16)
                if h == 0:
                    bias_s[rows, :] = jnp.where(dead, DEAD, unread)
                v_s[h, rows, :] = ref[at, image >> 4, :, 1, h].reshape(IMAGE_TOKENS, HEAD_WIDTH)

        for group, here in ((own, mine), (sib, jnp.logical_not(mine))):
            soon = jnp.logical_not(late)
            at = jnp.where(rel < 3, rel, rel - 3)
            pl.when(here & soon)(functools.partial(fetch, group[0], at))
            pl.when(here & late)(functools.partial(fetch, group[1], rel - 3))
    for h in range(heads):
        kt_s[h] = k_s[h].T
        vt_s[h] = v_s[h].T

    N = 2
    bias = jnp.concatenate([bias_s[...]] * N, axis=1)

    def load(ref, i):
        cols = [slice((N * i + n) * HEAD_WIDTH, (N * i + n + 1) * HEAD_WIDTH) for n in range(N)]
        return jnp.concatenate([ref[:, c] for c in cols], axis=0)

    def front(i):
        h = N * i // GROUP
        return mm(k_s[h], load(q_ref, i), 1, 1), mm(v_s[h], load(g_ref, i), 1, 1)

    def middle(s, dp):
        t = s * (SCALE * LOG2E) + bias
        e = jnp.exp2(t - jnp.max(t, axis=0, keepdims=True))
        p = e * (1.0 / jnp.sum(e, axis=0, keepdims=True))
        delta = jnp.sum(p * dp, axis=0, keepdims=True)
        return p.astype(bf16), (p * (dp - delta)).astype(bf16)

    def back(i, pb, ds):
        h = N * i // GROUP
        o = mm(vt_s[h], pb, 1, 0).astype(bf16).T
        dq = (mm(kt_s[h], ds, 1, 0) * SCALE).astype(bf16).T
        for n in range(N):
            cols = slice((N * i + n) * HEAD_WIDTH, (N * i + n + 1) * HEAD_WIDTH)
            att_ref[:, cols] = o[n * ROWS : (n + 1) * ROWS]
            dq_ref[:, cols] = dq[n * ROWS : (n + 1) * ROWS]
        dk, dv = mm(ds, load(q_ref, i), 1, 0), mm(pb, load(g_ref, i), 1, 0)
        if N * i % GROUP == 0:
            dk_s[b, h], dv_s[b, h] = dk, dv
        else:
            dk_s[b, h] += dk
            dv_s[b, h] += dv

    def clear(i):
        for ref in (gown_ref, gsoon_ref, glate_ref):
            part = ref.shape[0] // blocks
            for j in range(part * i // steps, part * (i + 1) // steps):
                ref[b * part + j] = jnp.zeros(ref.shape[1:], ref.dtype)

    steps = heads * GROUP // N
    ahead, behind = front(0), None
    for i in range(steps):
        clear(i)
        now, ahead = ahead, front(i + 1) if i + 1 < steps else None
        back(i, *middle(*now))

    @pl.when(b == blocks - 1)
    def _():
        for n in range(blocks * MAX_BLOCK_READS):
            block, r = divmod(n, MAX_BLOCK_READS)
            image = images[block, r]
            mine = (image & 1) == c
            rel = ((image >> 1) + Z - z) & (Z - 1)
            row = image >> 4
            rows = pl.ds(r * IMAGE_TOKENS, IMAGE_TOKENS)

            def add(ref, at, block=block, rows=rows):
                tile = (M, IMAGE_TOKENS // M, HEAD_WIDTH)
                for h in range(heads):
                    dk = (dk_s[block, h, rows, :] * SCALE).reshape(tile)
                    dv = dv_s[block, h, rows, :].reshape(tile)
                    ref[at, :, 0, h] = (ref[at, :, 0, h].astype(f32) + dk).astype(bf16)
                    ref[at, :, 1, h] = (ref[at, :, 1, h].astype(f32) + dv).astype(bf16)

            other = jnp.logical_not(mine)
            late = (rel < 3) | (rel > 5)
            at = jnp.where(rel < 3, rel, rel - 3) * Y + row
            pl.when(mine)(functools.partial(add, gown_ref, rel * Y + row))
            pl.when(other & late)(functools.partial(add, glate_ref, at))
            pl.when(other & jnp.logical_not(late))(functools.partial(add, gsoon_ref, (rel - 3) * Y + row))


def attend(images, reads, pos, query, gradient, own, sib):
    blocks = images.shape[0]
    heads = query.shape[1] // (GROUP * HEAD_WIDTH)
    smem = pl.BlockSpec(memory_space=pltpu.SMEM)
    whole = pl.BlockSpec(memory_space=pltpu.VMEM)
    text = pl.BlockSpec((ROWS, query.shape[1]), lambda b: (b, 0))
    pairs = blocks * heads * GROUP * ROWS * KEYS
    unit = own[0].shape[2:]
    return pl.pallas_call(
        attend_kernel,
        grid=(blocks,),
        in_specs=[smem] * 3 + [text] * 2 + [whole] * 4,
        out_specs=[text] * 2 + [whole] * 3,
        out_shape=[
            jax.ShapeDtypeStruct(query.shape, bf16),
            jax.ShapeDtypeStruct(query.shape, bf16),
            jax.ShapeDtypeStruct((Y * Z,) + unit, bf16),
            jax.ShapeDtypeStruct((3 * Y,) + unit, bf16),
            jax.ShapeDtypeStruct((5 * Y,) + unit, bf16),
        ],
        scratch_shapes=[
            pltpu.VMEM((heads, KEYS, HEAD_WIDTH), bf16),
            pltpu.VMEM((heads, KEYS, HEAD_WIDTH), bf16),
            pltpu.VMEM((heads, HEAD_WIDTH, KEYS), bf16),
            pltpu.VMEM((heads, HEAD_WIDTH, KEYS), bf16),
            pltpu.VMEM((KEYS, HEAD_WIDTH), f32),
            pltpu.VMEM((blocks, heads, KEYS, HEAD_WIDTH), f32),
            pltpu.VMEM((blocks, heads, KEYS, HEAD_WIDTH), f32),
        ],
        compiler_params=pltpu.CompilerParams(
            dimension_semantics=("arbitrary",), vmem_limit_bytes=40 * 2**20
        ),
        cost_estimate=pl.CostEstimate(
            flops=12 * HEAD_WIDTH * pairs, bytes_accessed=12 * 2**20, transcendentals=pairs
        ),
    )(images, reads, pos, query, gradient, *own, *sib)


def shift(x, axis, size, by):
    return lax.ppermute(x, axis, [(i, (i + by) % size) for i in range(size)])


def swap(x):
    return shift(x, "c", 2, 1)


def add(*terms):
    return sum(t.astype(f32) for t in terms).astype(bf16)


def gather_z(unit):
    half = unit.shape[0] // 2
    up, down = [unit], [unit]
    for _ in range(3):
        up.append(shift(up[-1], "z", Z, 1))
        down.append(shift(down[-1], "z", Z, -1))
    far = jnp.concatenate([shift(up[3][:half], "z", Z, 1), shift(down[3][half:], "z", Z, -1)])
    return jnp.stack([unit, down[1], down[2], up[2], up[1]]), jnp.stack([down[3], far, up[3]])


def reduce_z(own, soon, late):
    half = Y // 2
    own, soon, late = (x.reshape((-1, Y) + x.shape[1:]) for x in (own, soon, late))

    def sides(a, b):
        return lax.optimization_barrier((shift(a, "z", Z, 1), shift(b, "z", Z, -1)))

    up, down = sides(add(own[4, :half], soon[1, :half]), add(own[4, half:], soon[1, half:]))
    up = jnp.concatenate([add(own[3, :half], soon[0, :half], up), add(own[3, half:], soon[0, half:])])
    down = jnp.concatenate([add(own[5, :half], soon[2, :half]), add(own[5, half:], soon[2, half:], down)])
    up, down = sides(up, down)
    up, down = sides(add(own[2], late[2], up), add(own[6], late[3], down))
    up, down = sides(add(own[1], late[1], up), add(own[7], late[4], down))
    return add(own[0], late[0], up, down)


def local(query, image_key_values, image_count, block_images, block_reads, output_gradient):
    pos = jnp.stack([lax.axis_index("z"), lax.axis_index("c")]).astype(jnp.int32)
    slots = image_key_values.shape[2]
    slot = lax.axis_index("mp") * slots + jnp.arange(slots, dtype=jnp.int32)
    dead = (slot >= image_count[0])[None, :, None] & (jnp.arange(2) == 0)[:, None, None]
    kv = jnp.where(dead, MARKER, image_key_values[:, 0]).astype(bf16)
    kv = kv.reshape(2, slots, M, 2, HEAD_WIDTH).transpose(2, 0, 3, 1, 4)
    kv = jnp.broadcast_to(kv[None], (Y,) + kv.shape).reshape((Y * M,) + kv.shape[1:])
    unit = lax.all_to_all(kv, ("y", "mp"), 0, 0, tiled=True)
    own = gather_z(unit.reshape((Y, M) + unit.shape[1:]))
    sib = [swap(u) for u in own]
    attended, grad_query, gown, gsoon, glate = attend(
        block_images, block_reads, pos, query, output_gradient, own, sib
    )
    soon = swap(gsoon)
    late = swap(lax.optimization_barrier((glate, soon))[0])
    total = reduce_z(gown, soon, late)
    total = total.reshape((Y * M,) + total.shape[2:])
    total = lax.all_to_all(total, ("y", "mp"), 0, 0, tiled=True)
    total = jnp.sum(total.reshape((Y, M) + total.shape[1:]).astype(f32), axis=0)
    grad_kv = total.transpose(1, 3, 0, 2, 4).reshape(image_key_values.shape)
    return attended, grad_query, grad_kv


def solution(mesh):
    fine = Mesh(np.asarray(mesh.devices).reshape(Y, Z, 2, M), SEQ + ("mp",))
    placed = (
        P(SEQ, "mp"),
        P(None, SEQ, "mp", None),
        P(SEQ),
        P(SEQ, None),
        P(SEQ),
        P(SEQ, "mp"),
    )
    return jax.shard_map(
        local,
        mesh=fine,
        in_specs=placed,
        out_specs=(P(SEQ, "mp"), P(SEQ, "mp"), P(None, SEQ, "mp", None)),
        check_vma=False,
    )
```

```python
import functools

import jax
import jax.numpy as jnp
import numpy as np
from jax import lax
from jax.experimental import pallas as pl
from jax.experimental.pallas import tpu as pltpu
from jax.sharding import Mesh, PartitionSpec as P

QUERY_HEADS = 64
KEY_VALUE_HEADS = 8
HEAD_WIDTH = 128
MAX_BLOCK_READS = 6
IMAGE_TOKENS = 64
GROUP = QUERY_HEADS // KEY_VALUE_HEADS
ROWS = 128
KEYS = MAX_BLOCK_READS * IMAGE_TOKENS
SCALE = HEAD_WIDTH**-0.5
LOG2E = 1.4426950408889634
MARKER = 2.0**20
DEAD = -1e30
SEQ = ("y", "z", "c")
Y, Z, M = 4, 8, 4

f32 = jnp.float32
bf16 = jnp.bfloat16


def mm(a, b, ca, cb):
    return lax.dot_general(a, b, (((ca,), (cb,)), ((), ())), preferred_element_type=f32)


def attend_kernel(images, reads, pos, q_ref, g_ref, *refs):
    own, sib = refs[:2], refs[2:4]
    att_ref, dq_ref, gown_ref, gsoon_ref, glate_ref = refs[4:9]
    k_s, v_s, kt_s, vt_s, bias_s, dk_s, dv_s = refs[9:]
    b = pl.program_id(0)
    blocks, heads = dk_s.shape[:2]
    z, c = pos[0], pos[1]

    for r in range(MAX_BLOCK_READS):
        image = images[b, r]
        mine = (image & 1) == c
        rel = ((image >> 1) + Z - z) & (Z - 1)
        rows = pl.ds(r * IMAGE_TOKENS, IMAGE_TOKENS)

        def fetch(ref, at, image=image, rows=rows, r=r):
            unread = jnp.where(r < reads[b], 0.0, DEAD)
            for h in range(heads):
                k = ref[at, image >> 4, :, 0, h].reshape(IMAGE_TOKENS, HEAD_WIDTH).astype(f32)
                dead = k > 0.5 * MARKER
                k_s[h, rows, :] = jnp.where(dead, 0.0, k).astype(bf16)
                if h == 0:
                    bias_s[rows, :] = jnp.where(dead, DEAD, unread)
                v_s[h, rows, :] = ref[at, image >> 4, :, 1, h].reshape(IMAGE_TOKENS, HEAD_WIDTH)

        early = (rel < 3) | (rel > 5)
        for group, here in ((own, mine), (sib, jnp.logical_not(mine))):
            pl.when(here & early)(functools.partial(fetch, group[0], jnp.where(rel < 3, rel, rel - 3)))
            pl.when(here & jnp.logical_not(early))(functools.partial(fetch, group[1], rel - 3))
    for h in range(heads):
        kt_s[h] = k_s[h].T
        vt_s[h] = v_s[h].T

    N = 2
    bias = jnp.concatenate([bias_s[...]] * N, axis=1)

    def load(ref, i):
        cols = [slice((N * i + n) * HEAD_WIDTH, (N * i + n + 1) * HEAD_WIDTH) for n in range(N)]
        return jnp.concatenate([ref[:, c] for c in cols], axis=0)

    def front(i):
        h = N * i // GROUP
        return mm(k_s[h], load(q_ref, i), 1, 1), mm(v_s[h], load(g_ref, i), 1, 1)

    def middle(s, dp):
        t = s * (SCALE * LOG2E) + bias
        e = jnp.exp2(t - jnp.max(t, axis=0, keepdims=True))
        p = e * (1.0 / jnp.sum(e, axis=0, keepdims=True))
        delta = jnp.sum(p * dp, axis=0, keepdims=True)
        return p.astype(bf16), (p * (dp - delta)).astype(bf16)

    def back(i, pb, ds):
        h = N * i // GROUP
        o = mm(vt_s[h], pb, 1, 0).astype(bf16).T
        dq = (mm(kt_s[h], ds, 1, 0) * SCALE).astype(bf16).T
        for n in range(N):
            cols = slice((N * i + n) * HEAD_WIDTH, (N * i + n + 1) * HEAD_WIDTH)
            att_ref[:, cols] = o[n * ROWS : (n + 1) * ROWS]
            dq_ref[:, cols] = dq[n * ROWS : (n + 1) * ROWS]
        dk, dv = mm(ds, load(q_ref, i), 1, 0), mm(pb, load(g_ref, i), 1, 0)
        if N * i % GROUP == 0:
            dk_s[b, h], dv_s[b, h] = dk, dv
        else:
            dk_s[b, h] += dk
            dv_s[b, h] += dv

    def clear(i):
        for ref in (gown_ref, gsoon_ref, glate_ref):
            part = ref.shape[0] // blocks
            for j in range(part * i // steps, part * (i + 1) // steps):
                ref[b * part + j] = jnp.zeros(ref.shape[1:], ref.dtype)

    steps = heads * GROUP // N
    ahead, behind = front(0), None
    for i in range(steps):
        clear(i)
        now, ahead = ahead, front(i + 1) if i + 1 < steps else None
        back(i, *middle(*now))

    @pl.when(b == blocks - 1)
    def _():
        for n in range(blocks * MAX_BLOCK_READS):
            block, r = divmod(n, MAX_BLOCK_READS)
            image = images[block, r]
            mine = (image & 1) == c
            rel = ((image >> 1) + Z - z) & (Z - 1)
            rel = jnp.where((z & 1) == 0, rel, Z - rel) & (Z - 1)
            row = image >> 4
            rows = pl.ds(r * IMAGE_TOKENS, IMAGE_TOKENS)

            def add(ref, at, block=block, rows=rows):
                tile = (M, IMAGE_TOKENS // M, HEAD_WIDTH)
                for h in range(heads):
                    dk = (dk_s[block, h, rows, :] * SCALE).reshape(tile)
                    dv = dv_s[block, h, rows, :].reshape(tile)
                    ref[at, :, 0, h] = (ref[at, :, 0, h].astype(f32) + dk).astype(bf16)
                    ref[at, :, 1, h] = (ref[at, :, 1, h].astype(f32) + dv).astype(bf16)

            other, soon = jnp.logical_not(mine), rel == Z // 2
            at = jnp.where(rel < Z // 2, rel, rel - 1) * Y + row
            pl.when(mine)(functools.partial(add, gown_ref, rel * Y + row))
            pl.when(other & soon)(functools.partial(add, gsoon_ref, row))
            pl.when(other & jnp.logical_not(soon))(functools.partial(add, glate_ref, at))


def attend(images, reads, pos, query, gradient, own, sib):
    blocks = images.shape[0]
    heads = query.shape[1] // (GROUP * HEAD_WIDTH)
    smem = pl.BlockSpec(memory_space=pltpu.SMEM)
    whole = pl.BlockSpec(memory_space=pltpu.VMEM)
    text = pl.BlockSpec((ROWS, query.shape[1]), lambda b: (b, 0))
    pairs = blocks * heads * GROUP * ROWS * KEYS
    unit = own[0].shape[2:]
    return pl.pallas_call(
        attend_kernel,
        grid=(blocks,),
        in_specs=[smem] * 3 + [text] * 2 + [whole] * 4,
        out_specs=[text] * 2 + [whole] * 3,
        out_shape=[
            jax.ShapeDtypeStruct(query.shape, bf16),
            jax.ShapeDtypeStruct(query.shape, bf16),
            jax.ShapeDtypeStruct((Y * Z,) + unit, bf16),
            jax.ShapeDtypeStruct((Y,) + unit, bf16),
            jax.ShapeDtypeStruct(((Z - 1) * Y,) + unit, bf16),
        ],
        scratch_shapes=[
            pltpu.VMEM((heads, KEYS, HEAD_WIDTH), bf16),
            pltpu.VMEM((heads, KEYS, HEAD_WIDTH), bf16),
            pltpu.VMEM((heads, HEAD_WIDTH, KEYS), bf16),
            pltpu.VMEM((heads, HEAD_WIDTH, KEYS), bf16),
            pltpu.VMEM((KEYS, HEAD_WIDTH), f32),
            pltpu.VMEM((blocks, heads, KEYS, HEAD_WIDTH), f32),
            pltpu.VMEM((blocks, heads, KEYS, HEAD_WIDTH), f32),
        ],
        compiler_params=pltpu.CompilerParams(
            dimension_semantics=("arbitrary",), vmem_limit_bytes=40 * 2**20
        ),
        cost_estimate=pl.CostEstimate(
            flops=12 * HEAD_WIDTH * pairs, bytes_accessed=12 * 2**20, transcendentals=pairs
        ),
    )(images, reads, pos, pltpu.with_memory_space_constraint(query, pltpu.HBM), pltpu.with_memory_space_constraint(gradient, pltpu.HBM), *own, *sib)


def shift(x, axis, size, by):
    return lax.ppermute(x, axis, [(i, (i + by) % size) for i in range(size)])


def swap(x):
    return shift(x, "c", 2, 1)


def add(*terms):
    return sum(t.astype(f32) for t in terms).astype(bf16)


def gather_z(unit):
    half = unit.shape[0] // 2
    up, down = [unit], [unit]
    for _ in range(3):
        up.append(shift(up[-1], "z", Z, 1))
        down.append(shift(down[-1], "z", Z, -1))
    far = jnp.concatenate([shift(up[3][:half], "z", Z, 1), shift(down[3][half:], "z", Z, -1)])
    return jnp.stack([unit, down[1], down[2], up[2], up[1]]), jnp.stack([down[3], far, up[3]])


def exchange(a, b):
    pairs = [[(z, (z + (1 if z % 2 == n else -1)) % Z) for z in range(Z)] for n in range(2)]
    return lax.optimization_barrier((lax.ppermute(a, "z", pairs[0]), lax.ppermute(b, "z", pairs[1])))


def reduce_z(own, soon, late):
    half = Y // 2
    own, late = (x.reshape((-1, Y) + x.shape[1:]) for x in (own, late))
    a, b = exchange(add(own[4, :half], soon[:half]), add(own[4, half:], soon[half:]))
    a, b = exchange(
        jnp.concatenate([add(own[3, :half], late[3, :half]), add(own[3, half:], late[3, half:], b)]),
        jnp.concatenate([add(own[5, :half], late[4, :half], a), add(own[5, half:], late[4, half:])]),
    )
    a, b = exchange(add(own[2], late[2], b), add(own[6], late[5], a))
    a, b = exchange(add(own[1], late[1], b), add(own[7], late[6], a))
    return add(own[0], late[0], a, b)


def local(query, image_key_values, image_count, block_images, block_reads, output_gradient):
    pos = jnp.stack([lax.axis_index("z"), lax.axis_index("c")]).astype(jnp.int32)
    slots = image_key_values.shape[2]
    slot = lax.axis_index("mp") * slots + jnp.arange(slots, dtype=jnp.int32)
    dead = (slot >= image_count[0])[None, :, None] & (jnp.arange(2) == 0)[:, None, None]
    kv = jnp.where(dead, MARKER, image_key_values[:, 0]).astype(bf16)
    kv = kv.reshape(2, slots, M, 2, HEAD_WIDTH).transpose(2, 0, 3, 1, 4)
    kv = jnp.broadcast_to(kv[None], (Y,) + kv.shape).reshape((Y * M,) + kv.shape[1:])
    unit = lax.all_to_all(kv, ("y", "mp"), 0, 0, tiled=True)
    own = gather_z(unit.reshape((Y, M) + unit.shape[1:]))
    sib = [swap(u) for u in own]
    attended, grad_query, gown, gsoon, glate = attend(
        block_images, block_reads, pos, query, output_gradient, own, sib
    )
    soon = swap(gsoon)
    late = swap(lax.optimization_barrier((glate, soon))[0])
    total = reduce_z(gown, soon, late)
    total = total.reshape((Y * M,) + total.shape[2:])
    total = lax.all_to_all(total, ("y", "mp"), 0, 0, tiled=True)
    total = jnp.sum(total.reshape((Y, M) + total.shape[1:]).astype(f32), axis=0)
    grad_kv = total.transpose(1, 3, 0, 2, 4).reshape(image_key_values.shape)
    return attended, grad_query, grad_kv


def solution(mesh):
    fine = Mesh(np.asarray(mesh.devices).reshape(Y, Z, 2, M), SEQ + ("mp",))
    placed = (
        P(SEQ, "mp"),
        P(None, SEQ, "mp", None),
        P(SEQ),
        P(SEQ, None),
        P(SEQ),
        P(SEQ, "mp"),
    )
    return jax.shard_map(
        local,
        mesh=fine,
        in_specs=placed,
        out_specs=(P(SEQ, "mp"), P(SEQ, "mp"), P(None, SEQ, "mp", None)),
        check_vma=False,
    )
```

```python
import functools

import jax
import jax.numpy as jnp
import numpy as np
from jax import lax
from jax.experimental import pallas as pl
from jax.experimental.pallas import tpu as pltpu
from jax.sharding import Mesh, PartitionSpec as P

QUERY_HEADS = 64
KEY_VALUE_HEADS = 8
HEAD_WIDTH = 128
MAX_BLOCK_READS = 6
IMAGE_TOKENS = 64
GROUP = QUERY_HEADS // KEY_VALUE_HEADS
ROWS = 128
KEYS = MAX_BLOCK_READS * IMAGE_TOKENS
SCALE = HEAD_WIDTH**-0.5
LOG2E = 1.4426950408889634
MARKER = 2.0**20
DEAD = -1e30
SEQ = ("y", "z", "c")
Y, Z, M = 4, 8, 4

f32 = jnp.float32
bf16 = jnp.bfloat16


def mm(a, b, ca, cb):
    return lax.dot_general(a, b, (((ca,), (cb,)), ((), ())), preferred_element_type=f32)


def attend_kernel(images, reads, pos, q_ref, g_ref, *refs):
    own, sib = refs[:2], refs[2:4]
    att_ref, dq_ref, gown_ref, gsoon_ref, glate_ref = refs[4:9]
    k_s, v_s, kt_s, vt_s, bias_s, dk_s, dv_s = refs[9:]
    b = pl.program_id(0)
    blocks, heads = dk_s.shape[:2]
    z, c = pos[0], pos[1]

    for r in range(MAX_BLOCK_READS):
        image = images[b, r]
        mine = (image & 1) == c
        rel = ((image >> 1) + Z - z) & (Z - 1)
        rows = pl.ds(r * IMAGE_TOKENS, IMAGE_TOKENS)

        def fetch(ref, at, image=image, rows=rows, r=r):
            unread = jnp.where(r < reads[b], 0.0, DEAD)
            for h in range(heads):
                k = ref[at, image >> 4, :, 0, h].reshape(IMAGE_TOKENS, HEAD_WIDTH).astype(f32)
                dead = k > 0.5 * MARKER
                k_s[h, rows, :] = jnp.where(dead, 0.0, k).astype(bf16)
                if h == 0:
                    bias_s[rows, :] = jnp.where(dead, DEAD, unread)
                v_s[h, rows, :] = ref[at, image >> 4, :, 1, h].reshape(IMAGE_TOKENS, HEAD_WIDTH)

        early = (rel < 3) | (rel > 5)
        for group, here in ((own, mine), (sib, jnp.logical_not(mine))):
            pl.when(here & early)(functools.partial(fetch, group[0], jnp.where(rel < 3, rel, rel - 3)))
            pl.when(here & jnp.logical_not(early))(functools.partial(fetch, group[1], rel - 3))
    for h in range(heads):
        kt_s[h] = k_s[h].T
        vt_s[h] = v_s[h].T

    N = 2
    bias = jnp.concatenate([bias_s[...]] * N, axis=1)

    def load(ref, i):
        cols = [slice((N * i + n) * HEAD_WIDTH, (N * i + n + 1) * HEAD_WIDTH) for n in range(N)]
        return jnp.concatenate([ref[:, c] for c in cols], axis=0)

    def front(i):
        h = N * i // GROUP
        return mm(k_s[h], load(q_ref, i), 1, 1), mm(v_s[h], load(g_ref, i), 1, 1)

    def middle(s, dp):
        t = s * (SCALE * LOG2E) + bias
        e = jnp.exp2(t - jnp.max(t, axis=0, keepdims=True))
        p = e * (1.0 / jnp.sum(e, axis=0, keepdims=True))
        delta = jnp.sum(p * dp, axis=0, keepdims=True)
        return p.astype(bf16), (p * (dp - delta)).astype(bf16)

    def back(i, pb, ds):
        h = N * i // GROUP
        o = mm(vt_s[h], pb, 1, 0).astype(bf16).T
        dq = (mm(kt_s[h], ds, 1, 0) * SCALE).astype(bf16).T
        for n in range(N):
            cols = slice((N * i + n) * HEAD_WIDTH, (N * i + n + 1) * HEAD_WIDTH)
            att_ref[:, cols] = o[n * ROWS : (n + 1) * ROWS]
            dq_ref[:, cols] = dq[n * ROWS : (n + 1) * ROWS]
        dk, dv = mm(ds, load(q_ref, i), 1, 0), mm(pb, load(g_ref, i), 1, 0)
        if N * i % GROUP == 0:
            dk_s[b, h], dv_s[b, h] = dk, dv
        else:
            dk_s[b, h] += dk
            dv_s[b, h] += dv

    def clear(i):
        for ref in (gown_ref, gsoon_ref, glate_ref):
            part = ref.shape[0] // blocks
            for j in range(part * i // steps, part * (i + 1) // steps):
                ref[b * part + j] = jnp.zeros(ref.shape[1:], ref.dtype)

    steps = heads * GROUP // N
    ahead, behind = front(0), None
    for i in range(steps):
        clear(i)
        now, ahead = ahead, front(i + 1) if i + 1 < steps else None
        back(i, *middle(*now))

    @pl.when(b == blocks - 1)
    def _():
        for n in range(blocks * MAX_BLOCK_READS):
            block, r = divmod(n, MAX_BLOCK_READS)
            image = images[block, r]
            mine = (image & 1) == c
            rel = ((image >> 1) + Z - z) & (Z - 1)
            rel = jnp.where((z & 1) == 0, rel, Z - rel) & (Z - 1)
            row = image >> 4
            rows = pl.ds(r * IMAGE_TOKENS, IMAGE_TOKENS)

            def add(ref, at, block=block, rows=rows):
                tile = (M, IMAGE_TOKENS // M, HEAD_WIDTH)
                for h in range(heads):
                    dk = (dk_s[block, h, rows, :] * SCALE).reshape(tile)
                    dv = dv_s[block, h, rows, :].reshape(tile)
                    ref[at, :, 0, h] = (ref[at, :, 0, h].astype(f32) + dk).astype(bf16)
                    ref[at, :, 1, h] = (ref[at, :, 1, h].astype(f32) + dv).astype(bf16)

            other, soon = jnp.logical_not(mine), rel == Z // 2
            at = jnp.where(rel < Z // 2, rel, rel - 1) * Y + row
            pl.when(mine)(functools.partial(add, gown_ref, rel * Y + row))
            pl.when(other & soon)(functools.partial(add, gsoon_ref, row))
            pl.when(other & jnp.logical_not(soon))(functools.partial(add, glate_ref, at))


def attend(images, reads, pos, query, gradient, own, sib):
    blocks = images.shape[0]
    heads = query.shape[1] // (GROUP * HEAD_WIDTH)
    smem = pl.BlockSpec(memory_space=pltpu.SMEM)
    whole = pl.BlockSpec(memory_space=pltpu.VMEM)
    text = pl.BlockSpec((ROWS, query.shape[1]), lambda b: (b, 0))
    pairs = blocks * heads * GROUP * ROWS * KEYS
    unit = own[0].shape[2:]
    return pl.pallas_call(
        attend_kernel,
        grid=(blocks,),
        in_specs=[smem] * 3 + [text] * 2 + [whole] * 4,
        out_specs=[text] * 2 + [whole] * 3,
        out_shape=[
            jax.ShapeDtypeStruct(query.shape, bf16),
            jax.ShapeDtypeStruct(query.shape, bf16),
            jax.ShapeDtypeStruct((Y * Z,) + unit, bf16),
            jax.ShapeDtypeStruct((Y,) + unit, bf16),
            jax.ShapeDtypeStruct(((Z - 1) * Y,) + unit, bf16),
        ],
        scratch_shapes=[
            pltpu.VMEM((heads, KEYS, HEAD_WIDTH), bf16),
            pltpu.VMEM((heads, KEYS, HEAD_WIDTH), bf16),
            pltpu.VMEM((heads, HEAD_WIDTH, KEYS), bf16),
            pltpu.VMEM((heads, HEAD_WIDTH, KEYS), bf16),
            pltpu.VMEM((KEYS, HEAD_WIDTH), f32),
            pltpu.VMEM((blocks, heads, KEYS, HEAD_WIDTH), f32),
            pltpu.VMEM((blocks, heads, KEYS, HEAD_WIDTH), f32),
        ],
        compiler_params=pltpu.CompilerParams(
            dimension_semantics=("arbitrary",), vmem_limit_bytes=40 * 2**20
        ),
        cost_estimate=pl.CostEstimate(
            flops=12 * HEAD_WIDTH * pairs, bytes_accessed=12 * 2**20, transcendentals=pairs
        ),
    )(images, reads, pos, pltpu.with_memory_space_constraint(query, pltpu.HBM), pltpu.with_memory_space_constraint(gradient, pltpu.HBM), *own, *sib)


def shift(x, axis, size, by):
    return lax.ppermute(x, axis, [(i, (i + by) % size) for i in range(size)])


def swap(x):
    return shift(x, "c", 2, 1)


def add(*terms):
    return sum(t.astype(f32) for t in terms).astype(bf16)


def gather_z(unit):
    half = unit.shape[0] // 2
    up, down = [unit], [unit]
    for _ in range(3):
        up.append(shift(up[-1], "z", Z, 1))
        down.append(shift(down[-1], "z", Z, -1))
    far = jnp.concatenate([shift(up[3][:half], "z", Z, 1), shift(down[3][half:], "z", Z, -1)])
    return jnp.stack([unit, down[1], down[2], up[2], up[1]]), jnp.stack([down[3], far, up[3]])


def exchange(a, b):
    pairs = [[(z, (z + (1 if z % 2 == n else -1)) % Z) for z in range(Z)] for n in range(2)]
    return lax.optimization_barrier((lax.ppermute(a, "z", pairs[0]), lax.ppermute(b, "z", pairs[1])))


def reduce_z(own, soon, late):
    half = Y // 2
    own, late = (x.reshape((-1, Y) + x.shape[1:]) for x in (own, late))
    a, b = exchange(add(own[4, :half], soon[:half]), add(own[4, half:], soon[half:]))
    a, b = exchange(
        jnp.concatenate([add(own[3, :half], late[3, :half]), add(own[3, half:], late[3, half:], b)]),
        jnp.concatenate([add(own[5, :half], late[4, :half], a), add(own[5, half:], late[4, half:])]),
    )
    a, b = exchange(add(own[2], late[2], b), add(own[6], late[5], a))
    a, b = exchange(add(own[1], late[1], b), add(own[7], late[6], a))
    return add(own[0], late[0], a, b)


def local(query, image_key_values, image_count, block_images, block_reads, output_gradient):
    pos = jnp.stack([lax.axis_index("z"), lax.axis_index("c")]).astype(jnp.int32)
    slots = image_key_values.shape[2]
    slot = lax.axis_index("mp") * slots + jnp.arange(slots, dtype=jnp.int32)
    dead = (slot >= image_count[0])[None, :, None] & (jnp.arange(2) == 0)[:, None, None]
    kv = jnp.where(dead, MARKER, image_key_values[:, 0]).astype(bf16)
    kv = jnp.stack([kv[:, :, n * HEAD_WIDTH : (n + 1) * HEAD_WIDTH] for n in range(2 * M)])
    kv = kv.reshape((M, 2) + kv.shape[1:]).swapaxes(1, 2)
    kv = jnp.broadcast_to(kv[None], (Y,) + kv.shape).reshape((Y * M,) + kv.shape[1:])
    unit = lax.all_to_all(kv, ("y", "mp"), 0, 0, tiled=True)
    own = gather_z(unit.reshape((Y, M) + unit.shape[1:]))
    sib = [swap(u) for u in own]
    attended, grad_query, gown, gsoon, glate = attend(
        block_images, block_reads, pos, query, output_gradient, own, sib
    )
    soon = swap(gsoon)
    late = swap(lax.optimization_barrier((glate, soon))[0])
    total = reduce_z(gown, soon, late)
    total = total.reshape((Y * M,) + total.shape[2:])
    total = lax.all_to_all(total, ("y", "mp"), 0, 0, tiled=True)
    total = jnp.sum(total.reshape((Y, M) + total.shape[1:]).astype(f32), axis=0)
    grad_kv = jnp.concatenate([total[n // 2, :, n % 2] for n in range(2 * M)], axis=-1)
    grad_kv = grad_kv.reshape(image_key_values.shape)
    return attended, grad_query, grad_kv


def solution(mesh):
    fine = Mesh(np.asarray(mesh.devices).reshape(Y, Z, 2, M), SEQ + ("mp",))
    placed = (
        P(SEQ, "mp"),
        P(None, SEQ, "mp", None),
        P(SEQ),
        P(SEQ, None),
        P(SEQ),
        P(SEQ, "mp"),
    )
    return jax.shard_map(
        local,
        mesh=fine,
        in_specs=placed,
        out_specs=(P(SEQ, "mp"), P(SEQ, "mp"), P(None, SEQ, "mp", None)),
        check_vma=False,
    )
```

```python
import functools

import jax
import jax.numpy as jnp
import numpy as np
from jax import lax
from jax.experimental import pallas as pl
from jax.experimental.pallas import tpu as pltpu
from jax.sharding import Mesh, PartitionSpec as P

QUERY_HEADS = 64
KEY_VALUE_HEADS = 8
HEAD_WIDTH = 128
MAX_BLOCK_READS = 6
IMAGE_TOKENS = 64
GROUP = QUERY_HEADS // KEY_VALUE_HEADS
ROWS = 128
KEYS = MAX_BLOCK_READS * IMAGE_TOKENS
SCALE = HEAD_WIDTH**-0.5
LOG2E = 1.4426950408889634
MARKER = 2.0**20
DEAD = -1e30
SEQ = ("y", "z", "c")
Y, Z, M = 4, 8, 4

f32 = jnp.float32
bf16 = jnp.bfloat16


def mm(a, b, ca, cb):
    return lax.dot_general(a, b, (((ca,), (cb,)), ((), ())), preferred_element_type=f32)


def attend_kernel(images, reads, pos, q_ref, g_ref, *refs):
    own, sib = refs[:2], refs[2:4]
    att_ref, dq_ref, gown_ref, gsoon_ref, glate_ref = refs[4:9]
    k_s, v_s, kt_s, vt_s, bias_s, dk_s, dv_s = refs[9:]
    b = pl.program_id(0)
    blocks, heads = dk_s.shape[:2]
    z, c = pos[0], pos[1]

    for r in range(MAX_BLOCK_READS):
        image = images[b, r]
        mine = (image & 1) == c
        rel = ((image >> 1) + Z - z) & (Z - 1)
        rows = pl.ds(r * IMAGE_TOKENS, IMAGE_TOKENS)

        def fetch(ref, at, image=image, rows=rows, r=r):
            unread = jnp.where(r < reads[b], 0.0, DEAD)
            for h in range(heads):
                k = ref[at, image >> 4, :, 0, h].reshape(IMAGE_TOKENS, HEAD_WIDTH).astype(f32)
                dead = k > 0.5 * MARKER
                k_s[h, rows, :] = jnp.where(dead, 0.0, k).astype(bf16)
                if h == 0:
                    bias_s[rows, :] = jnp.where(dead, DEAD, unread)
                v_s[h, rows, :] = ref[at, image >> 4, :, 1, h].reshape(IMAGE_TOKENS, HEAD_WIDTH)

        early = (rel < 3) | (rel > 5)
        for group, here in ((own, mine), (sib, jnp.logical_not(mine))):
            pl.when(here & early)(functools.partial(fetch, group[0], jnp.where(rel < 3, rel, rel - 3)))
            pl.when(here & jnp.logical_not(early))(functools.partial(fetch, group[1], rel - 3))
    for h in range(heads):
        kt_s[h] = k_s[h].T
        vt_s[h] = v_s[h].T

    N = 2
    bias = jnp.concatenate([bias_s[...]] * N, axis=1)

    def load(ref, i):
        cols = [slice((N * i + n) * HEAD_WIDTH, (N * i + n + 1) * HEAD_WIDTH) for n in range(N)]
        return jnp.concatenate([ref[:, c] for c in cols], axis=0)

    def front(i):
        h = N * i // GROUP
        return mm(k_s[h], load(q_ref, i), 1, 1), mm(v_s[h], load(g_ref, i), 1, 1)

    def middle(s, dp):
        t = s * (SCALE * LOG2E) + bias
        e = jnp.exp2(t - jnp.max(t, axis=0, keepdims=True))
        p = e * (1.0 / jnp.sum(e, axis=0, keepdims=True))
        delta = jnp.sum(p * dp, axis=0, keepdims=True)
        return p.astype(bf16), (p * (dp - delta)).astype(bf16)

    def back(i, pb, ds):
        h = N * i // GROUP
        o = mm(vt_s[h], pb, 1, 0).astype(bf16).T
        dq = (mm(kt_s[h], ds, 1, 0) * SCALE).astype(bf16).T
        for n in range(N):
            cols = slice((N * i + n) * HEAD_WIDTH, (N * i + n + 1) * HEAD_WIDTH)
            att_ref[:, cols] = o[n * ROWS : (n + 1) * ROWS]
            dq_ref[:, cols] = dq[n * ROWS : (n + 1) * ROWS]
        dk, dv = mm(ds, load(q_ref, i), 1, 0), mm(pb, load(g_ref, i), 1, 0)
        if N * i % GROUP == 0:
            dk_s[b, h], dv_s[b, h] = dk, dv
        else:
            dk_s[b, h] += dk
            dv_s[b, h] += dv

    def clear(i):
        for ref in (gown_ref, gsoon_ref, glate_ref):
            part = ref.shape[0] // blocks
            for j in range(part * i // steps, part * (i + 1) // steps):
                ref[b * part + j] = jnp.zeros(ref.shape[1:], ref.dtype)

    steps = heads * GROUP // N
    ahead, behind = front(0), None
    for i in range(steps):
        clear(i)
        now, ahead = ahead, front(i + 1) if i + 1 < steps else None
        if behind is not None:
            back(i - 1, *behind)
        behind = middle(*now)
    back(steps - 1, *behind)

    @pl.when(b == blocks - 1)
    def _():
        for n in range(blocks * MAX_BLOCK_READS):
            block, r = divmod(n, MAX_BLOCK_READS)
            image = images[block, r]
            mine = (image & 1) == c
            rel = ((image >> 1) + Z - z) & (Z - 1)
            rel = jnp.where((z & 1) == 0, rel, Z - rel) & (Z - 1)
            row = image >> 4
            rows = pl.ds(r * IMAGE_TOKENS, IMAGE_TOKENS)

            def add(ref, at, block=block, rows=rows):
                tile = (M, IMAGE_TOKENS // M, HEAD_WIDTH)
                for h in range(heads):
                    dk = (dk_s[block, h, rows, :] * SCALE).reshape(tile)
                    dv = dv_s[block, h, rows, :].reshape(tile)
                    ref[at, :, 0, h] = (ref[at, :, 0, h].astype(f32) + dk).astype(bf16)
                    ref[at, :, 1, h] = (ref[at, :, 1, h].astype(f32) + dv).astype(bf16)

            other, soon = jnp.logical_not(mine), rel == Z // 2
            at = jnp.where(rel < Z // 2, rel, rel - 1) * Y + row
            pl.when(mine)(functools.partial(add, gown_ref, rel * Y + row))
            pl.when(other & soon)(functools.partial(add, gsoon_ref, row))
            pl.when(other & jnp.logical_not(soon))(functools.partial(add, glate_ref, at))


def attend(images, reads, pos, query, gradient, own, sib):
    blocks = images.shape[0]
    heads = query.shape[1] // (GROUP * HEAD_WIDTH)
    smem = pl.BlockSpec(memory_space=pltpu.SMEM)
    whole = pl.BlockSpec(memory_space=pltpu.VMEM)
    text = pl.BlockSpec((ROWS, query.shape[1]), lambda b: (b, 0))
    pairs = blocks * heads * GROUP * ROWS * KEYS
    unit = own[0].shape[2:]
    return pl.pallas_call(
        attend_kernel,
        grid=(blocks,),
        in_specs=[smem] * 3 + [text] * 2 + [whole] * 4,
        out_specs=[text] * 2 + [whole] * 3,
        out_shape=[
            jax.ShapeDtypeStruct(query.shape, bf16),
            jax.ShapeDtypeStruct(query.shape, bf16),
            jax.ShapeDtypeStruct((Y * Z,) + unit, bf16),
            jax.ShapeDtypeStruct((Y,) + unit, bf16),
            jax.ShapeDtypeStruct(((Z - 1) * Y,) + unit, bf16),
        ],
        scratch_shapes=[
            pltpu.VMEM((heads, KEYS, HEAD_WIDTH), bf16),
            pltpu.VMEM((heads, KEYS, HEAD_WIDTH), bf16),
            pltpu.VMEM((heads, HEAD_WIDTH, KEYS), bf16),
            pltpu.VMEM((heads, HEAD_WIDTH, KEYS), bf16),
            pltpu.VMEM((KEYS, HEAD_WIDTH), f32),
            pltpu.VMEM((blocks, heads, KEYS, HEAD_WIDTH), f32),
            pltpu.VMEM((blocks, heads, KEYS, HEAD_WIDTH), f32),
        ],
        compiler_params=pltpu.CompilerParams(
            dimension_semantics=("arbitrary",), vmem_limit_bytes=40 * 2**20
        ),
        cost_estimate=pl.CostEstimate(
            flops=12 * HEAD_WIDTH * pairs, bytes_accessed=12 * 2**20, transcendentals=pairs
        ),
    )(images, reads, pos, pltpu.with_memory_space_constraint(query, pltpu.HBM), pltpu.with_memory_space_constraint(gradient, pltpu.HBM), *own, *sib)


def shift(x, axis, size, by):
    return lax.ppermute(x, axis, [(i, (i + by) % size) for i in range(size)])


def swap(x):
    return shift(x, "c", 2, 1)


def add(*terms):
    return sum(t.astype(f32) for t in terms).astype(bf16)


def gather_z(unit):
    half = unit.shape[0] // 2
    up, down = [unit], [unit]
    for _ in range(3):
        up.append(shift(up[-1], "z", Z, 1))
        down.append(shift(down[-1], "z", Z, -1))
    far = jnp.concatenate([shift(up[3][:half], "z", Z, 1), shift(down[3][half:], "z", Z, -1)])
    return jnp.stack([unit, down[1], down[2], up[2], up[1]]), jnp.stack([down[3], far, up[3]])


def exchange(a, b):
    pairs = [[(z, (z + (1 if z % 2 == n else -1)) % Z) for z in range(Z)] for n in range(2)]
    return lax.optimization_barrier((lax.ppermute(a, "z", pairs[0]), lax.ppermute(b, "z", pairs[1])))


def reduce_z(own, soon, late):
    half = Y // 2
    own, late = (x.reshape((-1, Y) + x.shape[1:]) for x in (own, late))
    a, b = exchange(add(own[4, :half], soon[:half]), add(own[4, half:], soon[half:]))
    a, b = exchange(
        jnp.concatenate([add(own[3, :half], late[3, :half]), add(own[3, half:], late[3, half:], b)]),
        jnp.concatenate([add(own[5, :half], late[4, :half], a), add(own[5, half:], late[4, half:])]),
    )
    a, b = exchange(add(own[2], late[2], b), add(own[6], late[5], a))
    a, b = exchange(add(own[1], late[1], b), add(own[7], late[6], a))
    return add(own[0], late[0], a, b)


def local(query, image_key_values, image_count, block_images, block_reads, output_gradient):
    pos = jnp.stack([lax.axis_index("z"), lax.axis_index("c")]).astype(jnp.int32)
    slots = image_key_values.shape[2]
    slot = lax.axis_index("mp") * slots + jnp.arange(slots, dtype=jnp.int32)
    dead = (slot >= image_count[0])[None, :, None] & (jnp.arange(2) == 0)[:, None, None]
    kv = jnp.where(dead, MARKER, image_key_values[:, 0]).astype(bf16)
    kv = jnp.stack([kv[:, :, n * HEAD_WIDTH : (n + 1) * HEAD_WIDTH] for n in range(2 * M)])
    kv = kv.reshape((M, 2) + kv.shape[1:]).swapaxes(1, 2)
    kv = jnp.broadcast_to(kv[None], (Y,) + kv.shape).reshape((Y * M,) + kv.shape[1:])
    unit = lax.all_to_all(kv, ("y", "mp"), 0, 0, tiled=True)
    own = gather_z(unit.reshape((Y, M) + unit.shape[1:]))
    sib = [swap(u) for u in own]
    attended, grad_query, gown, gsoon, glate = attend(
        block_images, block_reads, pos, query, output_gradient, own, sib
    )
    soon = swap(gsoon)
    late = swap(lax.optimization_barrier((glate, soon))[0])
    total = reduce_z(gown, soon, late)
    total = total.reshape((Y * M,) + total.shape[2:])
    total = lax.all_to_all(total, ("y", "mp"), 0, 0, tiled=True)
    total = jnp.sum(total.reshape((Y, M) + total.shape[1:]).astype(f32), axis=0)
    grad_kv = jnp.concatenate([total[n // 2, :, n % 2] for n in range(2 * M)], axis=-1)
    grad_kv = grad_kv.reshape(image_key_values.shape)
    return attended, grad_query, grad_kv


def solution(mesh):
    fine = Mesh(np.asarray(mesh.devices).reshape(Y, Z, 2, M), SEQ + ("mp",))
    placed = (
        P(SEQ, "mp"),
        P(None, SEQ, "mp", None),
        P(SEQ),
        P(SEQ, None),
        P(SEQ),
        P(SEQ, "mp"),
    )
    return jax.shard_map(
        local,
        mesh=fine,
        in_specs=placed,
        out_specs=(P(SEQ, "mp"), P(SEQ, "mp"), P(None, SEQ, "mp", None)),
        check_vma=False,
    )
```

```python
import functools

import jax
import jax.numpy as jnp
import numpy as np
from jax import lax
from jax.experimental import pallas as pl
from jax.experimental.pallas import tpu as pltpu
from jax.sharding import Mesh, PartitionSpec as P

QUERY_HEADS = 64
KEY_VALUE_HEADS = 8
HEAD_WIDTH = 128
MAX_BLOCK_READS = 6
IMAGE_TOKENS = 64
GROUP = QUERY_HEADS // KEY_VALUE_HEADS
ROWS = 128
KEYS = MAX_BLOCK_READS * IMAGE_TOKENS
SCALE = HEAD_WIDTH**-0.5
LOG2E = 1.4426950408889634
MARKER = 2.0**20
DEAD = -1e30
SEQ = ("y", "z", "c")
Y, Z, M = 4, 8, 4

f32 = jnp.float32
bf16 = jnp.bfloat16


def mm(a, b, ca, cb):
    return lax.dot_general(a, b, (((ca,), (cb,)), ((), ())), preferred_element_type=f32)


def attend_kernel(images, reads, pos, q_ref, g_ref, *refs):
    own, sib = refs[:2], refs[2:4]
    att_ref, dq_ref, gown_ref, gsoon_ref, glate_ref = refs[4:9]
    k_s, v_s, kt_s, vt_s, bias_s, dk_s, dv_s = refs[9:]
    b = pl.program_id(0)
    blocks, heads = dk_s.shape[:2]
    z, c = pos[0], pos[1]

    for r in range(MAX_BLOCK_READS):
        image = images[b, r]
        mine = (image & 1) == c
        rel = ((image >> 1) + Z - z) & (Z - 1)
        rows = pl.ds(r * IMAGE_TOKENS, IMAGE_TOKENS)

        def fetch(ref, at, image=image, rows=rows, r=r):
            unread = jnp.where(r < reads[b], 0.0, DEAD)
            for h in range(heads):
                k = ref[at, image >> 4, :, 0, h].reshape(IMAGE_TOKENS, HEAD_WIDTH).astype(f32)
                dead = k > 0.5 * MARKER
                k_s[h, rows, :] = jnp.where(dead, 0.0, k).astype(bf16)
                if h == 0:
                    bias_s[rows, :] = jnp.where(dead, DEAD, unread)
                v_s[h, rows, :] = ref[at, image >> 4, :, 1, h].reshape(IMAGE_TOKENS, HEAD_WIDTH)

        early = (rel < 3) | (rel > 5)
        for group, here in ((own, mine), (sib, jnp.logical_not(mine))):
            pl.when(here & early)(functools.partial(fetch, group[0], jnp.where(rel < 3, rel, rel - 3)))
            pl.when(here & jnp.logical_not(early))(functools.partial(fetch, group[1], rel - 3))
    for h in range(heads):
        kt_s[h] = k_s[h].T
        vt_s[h] = v_s[h].T

    N = 2
    bias = jnp.concatenate([bias_s[...]] * N, axis=1)

    def load(ref, i):
        cols = [slice((N * i + n) * HEAD_WIDTH, (N * i + n + 1) * HEAD_WIDTH) for n in range(N)]
        return jnp.concatenate([ref[:, c] for c in cols], axis=0)

    def front(i):
        h = N * i // GROUP
        return mm(k_s[h], load(q_ref, i), 1, 1), mm(v_s[h], load(g_ref, i), 1, 1)

    def middle(s, dp):
        t = s * (SCALE * LOG2E) + bias
        e = jnp.exp2(t - jnp.max(t, axis=0, keepdims=True))
        p = e * (1.0 / jnp.sum(e, axis=0, keepdims=True))
        delta = jnp.sum(p * dp, axis=0, keepdims=True)
        return p.astype(bf16), (p * (dp - delta)).astype(bf16)

    def back(i, pb, ds):
        h = N * i // GROUP
        o = mm(vt_s[h], pb, 1, 0).astype(bf16).T
        dq = (mm(kt_s[h], ds, 1, 0) * SCALE).astype(bf16).T
        for n in range(N):
            cols = slice((N * i + n) * HEAD_WIDTH, (N * i + n + 1) * HEAD_WIDTH)
            att_ref[:, cols] = o[n * ROWS : (n + 1) * ROWS]
            dq_ref[:, cols] = dq[n * ROWS : (n + 1) * ROWS]
        dk, dv = mm(ds, load(q_ref, i), 1, 0), mm(pb, load(g_ref, i), 1, 0)
        if N * i % GROUP == 0:
            dk_s[b, h], dv_s[b, h] = dk, dv
        else:
            dk_s[b, h] += dk
            dv_s[b, h] += dv

    def clear(i):
        for ref in (gown_ref, gsoon_ref, glate_ref):
            part = ref.shape[0] // blocks
            for j in range(part * i // steps, part * (i + 1) // steps):
                ref[b * part + j] = jnp.zeros(ref.shape[1:], ref.dtype)

    steps = heads * GROUP // N
    ahead, behind = front(0), None
    for i in range(steps):
        clear(i)
        if behind is not None:
            back(i - 1, *behind)
        now, ahead = ahead, front(i + 1) if i + 1 < steps else None
        behind = middle(*now)
    back(steps - 1, *behind)

    @pl.when(b == blocks - 1)
    def _():
        for n in range(blocks * MAX_BLOCK_READS):
            block, r = divmod(n, MAX_BLOCK_READS)
            image = images[block, r]
            mine = (image & 1) == c
            rel = ((image >> 1) + Z - z) & (Z - 1)
            rel = jnp.where((z & 1) == 0, rel, Z - rel) & (Z - 1)
            row = image >> 4
            rows = pl.ds(r * IMAGE_TOKENS, IMAGE_TOKENS)

            def add(ref, at, block=block, rows=rows):
                tile = (M, IMAGE_TOKENS // M, HEAD_WIDTH)
                for h in range(heads):
                    dk = (dk_s[block, h, rows, :] * SCALE).reshape(tile)
                    dv = dv_s[block, h, rows, :].reshape(tile)
                    ref[at, :, 0, h] = (ref[at, :, 0, h].astype(f32) + dk).astype(bf16)
                    ref[at, :, 1, h] = (ref[at, :, 1, h].astype(f32) + dv).astype(bf16)

            other, soon = jnp.logical_not(mine), rel == Z // 2
            at = jnp.where(rel < Z // 2, rel, rel - 1) * Y + row
            pl.when(mine)(functools.partial(add, gown_ref, rel * Y + row))
            pl.when(other & soon)(functools.partial(add, gsoon_ref, row))
            pl.when(other & jnp.logical_not(soon))(functools.partial(add, glate_ref, at))


def attend(images, reads, pos, query, gradient, own, sib):
    blocks = images.shape[0]
    heads = query.shape[1] // (GROUP * HEAD_WIDTH)
    smem = pl.BlockSpec(memory_space=pltpu.SMEM)
    whole = pl.BlockSpec(memory_space=pltpu.VMEM)
    text = pl.BlockSpec((ROWS, query.shape[1]), lambda b: (b, 0))
    pairs = blocks * heads * GROUP * ROWS * KEYS
    unit = own[0].shape[2:]
    return pl.pallas_call(
        attend_kernel,
        grid=(blocks,),
        in_specs=[smem] * 3 + [text] * 2 + [whole] * 4,
        out_specs=[text] * 2 + [whole] * 3,
        out_shape=[
            jax.ShapeDtypeStruct(query.shape, bf16),
            jax.ShapeDtypeStruct(query.shape, bf16),
            jax.ShapeDtypeStruct((Y * Z,) + unit, bf16),
            jax.ShapeDtypeStruct((Y,) + unit, bf16),
            jax.ShapeDtypeStruct(((Z - 1) * Y,) + unit, bf16),
        ],
        scratch_shapes=[
            pltpu.VMEM((heads, KEYS, HEAD_WIDTH), bf16),
            pltpu.VMEM((heads, KEYS, HEAD_WIDTH), bf16),
            pltpu.VMEM((heads, HEAD_WIDTH, KEYS), bf16),
            pltpu.VMEM((heads, HEAD_WIDTH, KEYS), bf16),
            pltpu.VMEM((KEYS, HEAD_WIDTH), f32),
            pltpu.VMEM((blocks, heads, KEYS, HEAD_WIDTH), f32),
            pltpu.VMEM((blocks, heads, KEYS, HEAD_WIDTH), f32),
        ],
        compiler_params=pltpu.CompilerParams(
            dimension_semantics=("arbitrary",), vmem_limit_bytes=40 * 2**20
        ),
        cost_estimate=pl.CostEstimate(
            flops=12 * HEAD_WIDTH * pairs, bytes_accessed=12 * 2**20, transcendentals=pairs
        ),
    )(images, reads, pos, pltpu.with_memory_space_constraint(query, pltpu.HBM), pltpu.with_memory_space_constraint(gradient, pltpu.HBM), *own, *sib)


def shift(x, axis, size, by):
    return lax.ppermute(x, axis, [(i, (i + by) % size) for i in range(size)])


def swap(x):
    return shift(x, "c", 2, 1)


def add(*terms):
    return sum(t.astype(f32) for t in terms).astype(bf16)


def gather_z(unit):
    half = unit.shape[0] // 2
    up, down = [unit], [unit]
    for _ in range(3):
        up.append(shift(up[-1], "z", Z, 1))
        down.append(shift(down[-1], "z", Z, -1))
    far = jnp.concatenate([shift(up[3][:half], "z", Z, 1), shift(down[3][half:], "z", Z, -1)])
    return jnp.stack([unit, down[1], down[2], up[2], up[1]]), jnp.stack([down[3], far, up[3]])


def exchange(a, b):
    pairs = [[(z, (z + (1 if z % 2 == n else -1)) % Z) for z in range(Z)] for n in range(2)]
    return lax.optimization_barrier((lax.ppermute(a, "z", pairs[0]), lax.ppermute(b, "z", pairs[1])))


def reduce_z(own, soon, late):
    half = Y // 2
    own, late = (x.reshape((-1, Y) + x.shape[1:]) for x in (own, late))
    a, b = exchange(add(own[4, :half], soon[:half]), add(own[4, half:], soon[half:]))
    a, b = exchange(
        jnp.concatenate([add(own[3, :half], late[3, :half]), add(own[3, half:], late[3, half:], b)]),
        jnp.concatenate([add(own[5, :half], late[4, :half], a), add(own[5, half:], late[4, half:])]),
    )
    a, b = exchange(add(own[2], late[2], b), add(own[6], late[5], a))
    a, b = exchange(add(own[1], late[1], b), add(own[7], late[6], a))
    return add(own[0], late[0], a, b)


def local(query, image_key_values, image_count, block_images, block_reads, output_gradient):
    pos = jnp.stack([lax.axis_index("z"), lax.axis_index("c")]).astype(jnp.int32)
    slots = image_key_values.shape[2]
    slot = lax.axis_index("mp") * slots + jnp.arange(slots, dtype=jnp.int32)
    dead = (slot >= image_count[0])[None, :, None] & (jnp.arange(2) == 0)[:, None, None]
    kv = jnp.where(dead, MARKER, image_key_values[:, 0]).astype(bf16)
    kv = jnp.stack([kv[:, :, n * HEAD_WIDTH : (n + 1) * HEAD_WIDTH] for n in range(2 * M)])
    kv = kv.reshape((M, 2) + kv.shape[1:]).swapaxes(1, 2)
    kv = jnp.broadcast_to(kv[None], (Y,) + kv.shape).reshape((Y * M,) + kv.shape[1:])
    unit = lax.all_to_all(kv, ("y", "mp"), 0, 0, tiled=True)
    own = gather_z(unit.reshape((Y, M) + unit.shape[1:]))
    sib = [swap(u) for u in own]
    attended, grad_query, gown, gsoon, glate = attend(
        block_images, block_reads, pos, query, output_gradient, own, sib
    )
    soon = swap(gsoon)
    late = swap(lax.optimization_barrier((glate, soon))[0])
    total = reduce_z(gown, soon, late)
    total = total.reshape((Y * M,) + total.shape[2:])
    total = lax.all_to_all(total, ("y", "mp"), 0, 0, tiled=True)
    total = jnp.sum(total.reshape((Y, M) + total.shape[1:]).astype(f32), axis=0)
    grad_kv = jnp.concatenate([total[n // 2, :, n % 2] for n in range(2 * M)], axis=-1)
    grad_kv = grad_kv.reshape(image_key_values.shape)
    return attended, grad_query, grad_kv


def solution(mesh):
    fine = Mesh(np.asarray(mesh.devices).reshape(Y, Z, 2, M), SEQ + ("mp",))
    placed = (
        P(SEQ, "mp"),
        P(None, SEQ, "mp", None),
        P(SEQ),
        P(SEQ, None),
        P(SEQ),
        P(SEQ, "mp"),
    )
    return jax.shard_map(
        local,
        mesh=fine,
        in_specs=placed,
        out_specs=(P(SEQ, "mp"), P(SEQ, "mp"), P(None, SEQ, "mp", None)),
        check_vma=False,
    )
```
